32 devices in a mesh: ctx: 16 (over z, y, x), cand: 2 (over core).
Axes of the slice: x: 2, y: 2, z: 4, core: 2. Of those that a mesh axis runs over, the one named last changes fastest.
Arguments:
- history: bfloat16 [2048, 1024], P('ctx', 'cand'), may hold values from -6 to 6
- head_weights: bfloat16 [1024, 4096], P(None, 'cand'), may hold values from -0.1875 to 0.1875
- merge_weights: bfloat16 [1024, 1024], P('cand'), may hold values from -0.1875 to 0.1875
- cand_table: bfloat16 [1024, 1024], P('cand'), may hold values from -6 to 6
- user_weights: bfloat16 [1024, 512], P('cand'), may hold values from -0.1875 to 0.1875
- item_weights: bfloat16 [1024, 512], replicated, may hold values from -0.1875 to 0.1875
- score_weights: float32 [512], replicated, may hold values from -0.4 to 0.4
- request_points: int32 [64], replicated, may hold values from 0 to 2047, as said below
- candidate_owner: int32 [64, 512], P('ctx'), may hold values from 0 to 1
- candidate_row: int32 [64, 512], P('ctx'), may hold values from 0 to 511
- relevance: int32 [64, 512], P('ctx'), may hold values from 0 to 3
Outputs:
- losses: float32 [64], P('ctx')
- history_grad: float32 [2048, 1024], P('ctx', 'cand')
- grad_heads: float32 [1024, 4096], P('ctx', 'cand')
- grad_merge: float32 [1024, 1024], P('cand', 'ctx')
The draws below stay inside these ranges and needn't reach their ends.
Inputs may be any that keep to these rules, and one draw needn't show every extreme that they name: `request_points`: the last request is made at the last position of the history.
All inputs are finite; a program needn't handle non-finite values.
Results may differ from the reference program's by a relative error of at most 0.012.
The reference program's roundings to bfloat16 on the way (of `x_low`, `project`, `weight`, `gated`, `layer_out`, `d_attended`, `d_logit` and `d_before`) count: a program that leaves them out, or rounds other values in their place, can miss the bound.
Values may be sent and summed in bfloat16 or wider, within the bound.
A program may use at most 64 MiB of HBM per device.

```python
import math
import jax
import jax.numpy as jnp
from jax import lax

D = 1024
HEADS = 8
HEAD = 128
NCAND = 512
HIDDEN_SIZE = 512
ROWS_DEV = 512
SEQ = 2048
REQUESTS = 64
ROWS = 1024
N_CAND = 2


def draw_request_points(key, part):
    key = jax.random.fold_in(key, 7)
    points = jax.random.randint(key, (REQUESTS,), 0, SEQ, dtype=jnp.int32)
    return points.at[REQUESTS - 1].set(SEQ - 1)


def set_ends(entries, stream_key, smallest, top_value):
    shape = entries.shape
    spot = [jax.random.randint(jax.random.fold_in(stream_key, axis), (), 0, shape[axis]) for axis in range(len(shape))]
    entries = entries.at[tuple(spot)].set(smallest)
    longest = shape.index(max(shape))
    spot[longest] = (spot[longest] + 1) % shape[longest]
    return entries.at[tuple(spot)].set(top_value)


def block_levels(rng, extent, split, smallest, largest):
    def one(dim, shards_of):
        draws = jax.random.uniform(jax.random.fold_in(jax.random.fold_in(rng, 6), dim), (shards_of,), jnp.float32, smallest / len(split), largest / len(split))
        return jnp.repeat(jnp.exp(draws), extent[dim] // shards_of).reshape((-1,) + (1,) * (len(extent) - dim - 1))

    loudness = one(*split[0])
    for cut in split[1:]:
        loudness = loudness * one(*cut)
    return loudness


def scatter_about(own_key, shape, scale, reach, cuts=(), held_as=jnp.bfloat16):
    factor_of = block_levels(own_key, shape, cuts, -0.22, 0.18) if cuts else 1.0
    array = jax.random.normal(own_key, shape, jnp.float32) * scale * factor_of
    return jnp.minimum(jnp.maximum(array, -reach), reach).astype(held_as)


def setup_inputs(seed: int = 0) -> dict:
    key_list = jax.random.split(jax.random.key(seed), 12)
    history = scatter_about(key_list[0], (SEQ, D), 1.0, 6.0, ((0, 16), (1, 2)))
    head_weights = scatter_about(key_list[1], (D, 4 * HEADS * HEAD), D ** -0.5, 0.1875, ((1, 2),))
    merge_weights = scatter_about(key_list[2], (HEADS * HEAD, D), (HEADS * HEAD) ** -0.5, 0.1875, ((0, 2),))
    cand_table = scatter_about(key_list[3], (ROWS, D), 1.0, 6.0, ((0, 2),))
    user_weights = scatter_about(key_list[4], (D, HIDDEN_SIZE), D ** -0.5, 0.1875, ((0, 2),))
    item_weights = scatter_about(key_list[5], (D, HIDDEN_SIZE), D ** -0.5, 0.1875)
    score_weights = scatter_about(key_list[6], (HIDDEN_SIZE,), 0.1, 0.4, (), jnp.float32)
    request_points = draw_request_points(jax.random.fold_in(key_list[11], 71), 0)
    candidate_owner = set_ends(jax.random.randint(key_list[8], (REQUESTS, NCAND), 0, N_CAND), jax.random.fold_in(key_list[8], 1), 0, N_CAND - 1).astype(jnp.int32)
    candidate_row = set_ends(jax.random.randint(key_list[9], (REQUESTS, NCAND), 0, ROWS_DEV), jax.random.fold_in(key_list[9], 1), 0, ROWS_DEV - 1).astype(jnp.int32)
    relevance = set_ends(jax.random.randint(key_list[10], (REQUESTS, NCAND), 0, 4), jax.random.fold_in(key_list[10], 1), 0, 3).astype(jnp.int32)
    return dict(history=history, head_weights=head_weights, merge_weights=merge_weights, cand_table=cand_table, user_weights=user_weights, item_weights=item_weights, score_weights=score_weights, request_points=request_points, candidate_owner=candidate_owner, candidate_row=candidate_row, relevance=relevance)


norm_eps = 1e-05

def silu_slope(argument):
    sigmoid_part = jax.nn.sigmoid(argument)
    return sigmoid_part * (1.0 + argument * (1.0 - sigmoid_part))

def layer_norm(argument):
    centred = argument - lax.optimization_barrier(jnp.mean(argument, -1, keepdims=True))
    inverse = lax.rsqrt(lax.optimization_barrier(jnp.mean(centred * centred, -1, keepdims=True)) + norm_eps)
    return (centred * inverse, inverse)

def norm_back(gradient, normed, inverse):
    return inverse * (gradient - lax.optimization_barrier(jnp.mean(gradient, -1, keepdims=True)) - normed * lax.optimization_barrier(jnp.mean(gradient * normed, -1, keepdims=True)))

def score_tile(queries, key_heads, query_start, key_start):
    scaling = queries.shape[-1] ** (-0.5)
    logits = jnp.dot(queries, key_heads.T, preferred_element_type=jnp.float32) * scaling
    query_place = query_start + jnp.arange(queries.shape[0], dtype=jnp.int32)
    key_place = key_start + jnp.arange(key_heads.shape[0], dtype=jnp.int32)
    allowed = key_place[None, :] <= query_place[:, None]
    divisor = (query_place + 1).astype(jnp.float32)[:, None]
    return (logits, allowed, divisor)

def head_forward(queries, key_heads, values):
    length = queries.shape[0]
    block_rows = math.gcd(512, length)
    starts = jnp.arange(0, length, block_rows, dtype=jnp.int32)

    def query_block(begin):
        block = lax.dynamic_slice_in_dim(queries, begin, block_rows, 0)
        logits, allowed, divisor = score_tile(block, key_heads, begin, 0)
        weight = jnp.where(allowed, jax.nn.silu(logits) / divisor, 0.0).astype(jnp.bfloat16)
        return jnp.dot(weight, values, preferred_element_type=jnp.float32)
    return lax.map(query_block, starts).reshape(length, queries.shape[1])

def head_backward(queries, key_heads, values, out_grads):
    length = queries.shape[0]
    block_rows = math.gcd(512, length)
    starts = jnp.arange(0, length, block_rows, dtype=jnp.int32)
    scaling = queries.shape[-1] ** (-0.5)

    def query_block(begin):
        block = lax.dynamic_slice_in_dim(queries, begin, block_rows, 0)
        grads_block = lax.dynamic_slice_in_dim(out_grads, begin, block_rows, 0)
        logits, allowed, divisor = score_tile(block, key_heads, begin, 0)
        slopes = jnp.dot(grads_block, values.T, preferred_element_type=jnp.float32)
        d_logit = jnp.where(allowed, slopes * silu_slope(logits) / divisor, 0.0).astype(jnp.bfloat16)
        return jnp.dot(d_logit, key_heads, preferred_element_type=jnp.float32) * scaling

    def key_block(begin):
        key_part = lax.dynamic_slice_in_dim(key_heads, begin, block_rows, 0)
        value_part = lax.dynamic_slice_in_dim(values, begin, block_rows, 0)
        logits, allowed, divisor = score_tile(queries, key_part, 0, begin)
        weight = jnp.where(allowed, jax.nn.silu(logits) / divisor, 0.0).astype(jnp.bfloat16)
        d_value = jnp.dot(weight.T, out_grads, preferred_element_type=jnp.float32)
        slopes = jnp.dot(out_grads, value_part.T, preferred_element_type=jnp.float32)
        d_logit = jnp.where(allowed, slopes * silu_slope(logits) / divisor, 0.0).astype(jnp.bfloat16)
        d_key = jnp.dot(d_logit.T, queries, preferred_element_type=jnp.float32) * scaling
        return (d_key, d_value)
    width = queries.shape[1]
    d_query = lax.map(query_block, starts).reshape(length, width)
    d_key, d_value = lax.map(key_block, starts)
    return (d_query, d_key.reshape(length, width), d_value.reshape(length, width))

def reference(history, head_weights, merge_weights, cand_table, user_weights, item_weights, score_weights, request_points, candidate_owner, candidate_row, relevance):
    length = history.shape[0]
    x_wide = history.astype(jnp.float32)
    x_normed, x_inverse = layer_norm(x_wide)
    x_low = x_normed.astype(jnp.bfloat16)
    before = jnp.dot(x_low, head_weights, preferred_element_type=jnp.float32)
    project = jax.nn.silu(before).astype(jnp.bfloat16)
    sections = project.reshape(length, HEADS, 4, HEAD).transpose(2, 1, 0, 3)
    gate_part, values, queries, key_heads = (sections[0], sections[1], sections[2], sections[3])
    attended = lax.map(lambda stacked: head_forward(stacked[0], stacked[1], stacked[2]), (queries, key_heads, values))
    normed, inverse = layer_norm(attended)
    gated = (normed * gate_part.astype(jnp.float32)).astype(jnp.bfloat16)
    gated_rows = gated.transpose(1, 0, 2).reshape(length, HEADS * HEAD)
    layer_out = (x_wide + jnp.dot(gated_rows, merge_weights, preferred_element_type=jnp.float32)).astype(jnp.bfloat16)
    picked = layer_out[request_points]
    user_proj = jnp.dot(picked, user_weights, preferred_element_type=jnp.float32)
    item_proj = jnp.dot(cand_table, item_weights, preferred_element_type=jnp.float32)
    row_index = (candidate_owner * ROWS_DEV + candidate_row).astype(jnp.int32)

    def request_scores(request):
        user_row, index_row, grade_row = request
        pre_score = user_row[None, :] + item_proj[index_row]
        scores = lax.optimization_barrier(jnp.sum(jax.nn.silu(pre_score) * score_weights[None, :], -1))
        log_total = jnp.log(jnp.sum(jnp.exp(scores)))
        target = (grade_row + 1).astype(jnp.float32)
        target = target / jnp.sum(target)
        request_loss = log_total - jnp.sum(target * scores)
        d_score = jnp.exp(scores - log_total) - target
        d_user = lax.optimization_barrier(jnp.sum(d_score[:, None] * score_weights[None, :] * silu_slope(pre_score), 0))
        return (request_loss, d_user)
    losses, d_user = lax.map(request_scores, (user_proj, row_index, relevance))
    d_picked = jnp.dot(d_user, user_weights.astype(jnp.float32).T, precision=lax.Precision.HIGHEST)
    d_layer = jnp.zeros((length, history.shape[1]), jnp.float32).at[request_points].add(d_picked)
    d_gated = jnp.dot(d_layer, merge_weights.astype(jnp.float32).T, precision=lax.Precision.HIGHEST)
    grad_merge = jnp.dot(gated_rows.astype(jnp.float32).T, d_layer, precision=lax.Precision.HIGHEST)
    d_gated = d_gated.reshape(length, HEADS, HEAD).transpose(1, 0, 2)
    d_gate = d_gated * normed
    d_attended = norm_back(d_gated * gate_part.astype(jnp.float32), normed, inverse).astype(jnp.bfloat16)
    d_query, d_key, d_value = lax.map(lambda stacked: head_backward(stacked[0], stacked[1], stacked[2], stacked[3]), (queries, key_heads, values, d_attended))
    d_project = jnp.stack([d_gate, d_value, d_query, d_key], 0).transpose(2, 1, 0, 3).reshape(length, 4 * HEADS * HEAD)
    d_before = (d_project * silu_slope(before)).astype(jnp.bfloat16)
    grad_heads = jnp.dot(x_low.T, d_before, preferred_element_type=jnp.float32)
    d_normed = jnp.dot(d_before, head_weights.T, preferred_element_type=jnp.float32)
    history_grad = d_layer + norm_back(d_normed, x_normed, x_inverse)
    return (losses, history_grad, grad_heads, grad_merge)
```

```python
import jax
import jax.numpy as jnp
from jax import lax
from jax.sharding import PartitionSpec as P

HEAD = 128
norm_eps = 1e-05
HIGHEST = lax.Precision.HIGHEST
F32 = jnp.float32
BF16 = jnp.bfloat16


def silu_slope(argument):
    sigmoid_part = jax.nn.sigmoid(argument)
    return sigmoid_part * (1.0 + argument * (1.0 - sigmoid_part))


def layer_norm(argument):
    centred = argument - jnp.mean(argument, -1, keepdims=True)
    inverse = lax.rsqrt(jnp.mean(centred * centred, -1, keepdims=True) + norm_eps)
    return (centred * inverse, inverse)


def norm_back(gradient, normed, inverse):
    return inverse * (
        gradient
        - jnp.mean(gradient, -1, keepdims=True)
        - normed * jnp.mean(gradient * normed, -1, keepdims=True)
    )


def mm(left, right):
    return jnp.dot(left, right, preferred_element_type=F32)


def gather_history(history):
    rows = lax.all_gather(history, "ctx", axis=0, tiled=True)
    return lax.all_gather(rows, "cand", axis=1, tiled=True)


def gather_user_grad(part):
    return lax.all_gather(lax.psum(part, "cand"), "ctx", axis=0, tiled=True)


def per_device(
    history,
    head_weights,
    merge_weights,
    cand_table,
    user_weights,
    item_weights,
    score_weights,
    request_points,
    candidate_owner,
    candidate_row,
    relevance,
):
    row_count, slice_width = history.shape
    width = head_weights.shape[0]
    ctx_index = lax.axis_index("ctx")
    cand_index = lax.axis_index("cand")
    ctx_count = lax.axis_size("ctx")
    first_row = ctx_index * row_count
    heads = merge_weights.shape[0] // HEAD
    cols = heads * HEAD
    requests = request_points.shape[0]
    own_requests = candidate_row.shape[0]
    scaling = HEAD ** (-0.5)

    sections = head_weights.reshape(width, heads, 4, HEAD)
    gate_w, value_w, query_w, key_w = (
        sections[:, :, index].reshape(width, cols) for index in range(4)
    )
    item_proj = mm(cand_table, item_weights)
    user_full = lax.all_gather(user_weights, "cand", axis=0, tiled=True)

    features = gather_history(history)
    length = features.shape[0]
    x_low = layer_norm(features.astype(F32))[0].astype(BF16)

    picks = (request_points[:, None] == jnp.arange(length, dtype=jnp.int32)[None, :]).astype(BF16)
    x_requests = mm(picks, x_low).astype(BF16)
    raw_requests = mm(picks, features)

    before_key = mm(x_low, key_w)
    before_value = mm(x_low, value_w)
    before_query = mm(x_requests, query_w)
    before_gate = mm(x_requests, gate_w)

    def split(array):
        return array.reshape(array.shape[0], heads, HEAD)

    key_heads = split(jax.nn.silu(before_key).astype(BF16))
    values = split(jax.nn.silu(before_value).astype(BF16))
    queries = split(jax.nn.silu(before_query).astype(BF16))
    gate_part = split(jax.nn.silu(before_gate).astype(BF16)).astype(F32)

    logits = jnp.einsum("qhd,khd->hqk", queries, key_heads, preferred_element_type=F32) * scaling
    allowed = (jnp.arange(length, dtype=jnp.int32)[None, :] <= request_points[:, None])[None]
    divisor = (request_points + 1).astype(F32)[None, :, None]
    weight = jnp.where(allowed, jax.nn.silu(logits) / divisor, 0.0).astype(BF16)
    attended = jnp.einsum("hqk,khd->qhd", weight, values, preferred_element_type=F32)
    normed, inverse = layer_norm(attended)
    gated = (normed * gate_part).astype(BF16).reshape(requests, cols)

    def own(array):
        return lax.dynamic_slice_in_dim(array, ctx_index * own_requests, own_requests, 0)

    head_total = lax.psum(mm(own(gated), merge_weights), "cand")
    layer_out = (own(raw_requests) + head_total).astype(BF16)
    user_proj = mm(layer_out, user_full)

    owned = candidate_owner == cand_index
    table_rows = jnp.arange(cand_table.shape[0], dtype=jnp.int32)
    hits = owned[:, :, None] & (candidate_row[:, :, None] == table_rows)
    pre_score = user_proj[:, None, :] + item_proj[None]
    row_scores = jnp.sum(jax.nn.silu(pre_score) * score_weights, -1)
    scores = lax.psum(jnp.sum(jnp.where(hits, row_scores[:, None, :], 0.0), -1), "cand")
    log_total = jnp.log(jnp.sum(jnp.exp(scores), -1, keepdims=True))
    target = (relevance + 1).astype(F32)
    target = target / jnp.sum(target, -1, keepdims=True)
    losses = log_total[:, 0] - jnp.sum(target * scores, -1)
    d_score = jnp.exp(scores - log_total) - target
    row_grads = jnp.sum(jnp.where(hits, d_score[:, :, None], 0.0), 1)
    user_part = jnp.sum(row_grads[:, :, None] * silu_slope(pre_score), 1) * score_weights
    d_user = gather_user_grad(user_part)

    same = request_points[:, None] == request_points[None, :]
    order = jnp.arange(requests, dtype=jnp.int32)
    earlier = jnp.any(same & (order[None, :] < order[:, None]), 1)
    merge_same = (same & ~earlier[:, None]).astype(F32)
    d_user = jnp.dot(merge_same, d_user, precision=HIGHEST)
    d_picked = jnp.dot(d_user, user_full.astype(F32).T, precision=HIGHEST)
    d_gated = split(jnp.dot(d_picked, merge_weights.astype(F32).T, precision=HIGHEST))
    d_gate = (d_gated * normed).reshape(requests, cols)
    d_attended = norm_back(d_gated * gate_part, normed, inverse).astype(BF16)

    merge_cols = width // ctx_count
    own_picked = lax.dynamic_slice_in_dim(d_picked, ctx_index * merge_cols, merge_cols, 1)
    grad_merge = lax.dot_general(
        gated.astype(F32), own_picked, (((0,), (0,)), ((), ())), precision=HIGHEST
    )

    slopes = jnp.einsum("qhd,khd->hqk", d_attended, values, preferred_element_type=F32)
    d_logit = jnp.where(allowed, slopes * silu_slope(logits) / divisor, 0.0).astype(BF16)
    d_query = jnp.einsum("hqk,khd->qhd", d_logit, key_heads, preferred_element_type=F32) * scaling
    d_key = jnp.einsum("hqk,qhd->khd", d_logit, queries, preferred_element_type=F32) * scaling
    d_value = jnp.einsum("hqk,qhd->khd", weight, d_attended, preferred_element_type=F32)

    d_before_key = (d_key.reshape(length, cols) * silu_slope(before_key)).astype(BF16)
    d_before_value = (d_value.reshape(length, cols) * silu_slope(before_value)).astype(BF16)
    d_before_query = (d_query.reshape(requests, cols) * silu_slope(before_query)).astype(BF16)
    d_before_gate = (d_gate * silu_slope(before_gate)).astype(BF16)

    def own_features(array):
        return lax.dynamic_slice_in_dim(array, ctx_index * merge_cols, merge_cols, 1)

    def grad_of(rows, grads):
        return split(lax.dot_general(rows, grads, (((0,), (0,)), ((), ())), preferred_element_type=F32))

    x_own = own_features(x_low)
    x_own_requests = own_features(x_requests)
    grad_heads = jnp.stack(
        [
            grad_of(x_own_requests, d_before_gate),
            grad_of(x_own, d_before_value),
            grad_of(x_own_requests, d_before_query),
            grad_of(x_own, d_before_key),
        ],
        2,
    ).reshape(merge_cols, 4 * cols)

    def own_rows(array):
        return lax.dynamic_slice_in_dim(array, first_row, row_count, 0)

    positions = first_row + jnp.arange(row_count, dtype=jnp.int32)
    places = positions[:, None] == request_points[None, :]
    low_places = places.astype(BF16)
    transposed = (((1,), (1,)), ((), ()))

    def back(grads, weights):
        return lax.dot_general(grads, weights, transposed, preferred_element_type=F32)

    d_normed = lax.psum(
        back(own_rows(d_before_key), key_w)
        + back(own_rows(d_before_value), value_w)
        + back(mm(low_places, d_before_query).astype(BF16), query_w)
        + back(mm(low_places, d_before_gate).astype(BF16), gate_w),
        "cand",
    )
    x_normed, x_inverse = layer_norm(own_rows(features).astype(F32))
    column_start = cand_index * slice_width
    d_input = lax.dynamic_slice_in_dim(
        norm_back(d_normed, x_normed, x_inverse), column_start, slice_width, 1
    )
    picked_cols = lax.dynamic_slice_in_dim(d_picked, column_start, slice_width, 1)
    d_layer = jnp.dot(places.astype(F32), picked_cols, precision=HIGHEST)
    history_grad = d_layer + d_input
    return (losses, history_grad, grad_heads, grad_merge)


def solution(mesh):
    return jax.shard_map(
        per_device,
        mesh=mesh,
        in_specs=(
            P("ctx", "cand"),
            P(None, "cand"),
            P("cand", None),
            P("cand", None),
            P("cand", None),
            P(),
            P(),
            P(),
            P("ctx", None),
            P("ctx", None),
            P("ctx", None),
        ),
        out_specs=(P("ctx"), P("ctx", "cand"), P("ctx", "cand"), P("cand", "ctx")),
        check_vma=False,
    )
```

```python
import functools

import jax
import jax.numpy as jnp
from jax import lax
from jax.experimental import pallas as pl
from jax.experimental.pallas import tpu as pltpu
from jax.sharding import PartitionSpec as P

HEAD = 128
norm_eps = 1e-05
HIGHEST = lax.Precision.HIGHEST
F32 = jnp.float32
BF16 = jnp.bfloat16


def silu_slope(argument):
    sigmoid_part = jax.nn.sigmoid(argument)
    return sigmoid_part * (1.0 + argument * (1.0 - sigmoid_part))


def layer_norm(argument):
    centred = argument - jnp.mean(argument, -1, keepdims=True)
    inverse = lax.rsqrt(jnp.mean(centred * centred, -1, keepdims=True) + norm_eps)
    return (centred * inverse, inverse)


def norm_back(gradient, normed, inverse):
    return inverse * (
        gradient
        - jnp.mean(gradient, -1, keepdims=True)
        - normed * jnp.mean(gradient * normed, -1, keepdims=True)
    )


def mm(left, right):
    return jnp.dot(left, right, preferred_element_type=F32)


MESH = pl.DeviceIdType.MESH
VMEM = pl.BlockSpec(memory_space=pltpu.VMEM)
DMA = pltpu.SemaphoreType.DMA


def kernel_params(collective_id):
    return pltpu.CompilerParams(
        collective_id=collective_id, has_side_effects=True, vmem_limit_bytes=48 * 1024 * 1024
    )


def flip(number, bits):
    place = 1
    result = number
    while place <= bits:
        if bits & place:
            result = result + place - 2 * place * ((number // place) % 2)
        place *= 2
    return result


def meet(peers):
    barrier = pltpu.get_barrier_semaphore()
    for peer in peers:
        pl.semaphore_signal(barrier, inc=1, device_id=peer, device_id_type=MESH)
    pl.semaphore_wait(barrier, len(peers))


def history_kernel(
    ctx_count,
    cand_count,
    history,
    user,
    features,
    user_full,
    line_send,
    first_send,
    second_send,
    cand_send,
    ctx_recv,
    cand_recv,
    user_send,
    user_recv,
):
    rows, slice_width = history.shape
    user_rows = user.shape[0]
    ctx = lax.axis_index("ctx")
    cand = lax.axis_index("cand")
    depth = ctx_count // 4
    line, low = ctx // 4, ctx % 4
    odd = cand % 2
    flip_x, flip_y = flip(ctx, 1), flip(ctx, 2)
    first = flip_x + odd * (flip_y - flip_x)
    second = flip_y + odd * (flip_x - flip_y)
    line_peers = [flip(line, step) * 4 + low for step in range(1, depth)]
    cand_peers = [(cand + step) % cand_count for step in range(1, cand_count)]
    meet(
        [(peer, cand) for peer in line_peers]
        + [(first, cand), (second, cand)]
        + [(ctx, peer) for peer in cand_peers]
    )
    columns = pl.ds(pl.multiple_of(cand * slice_width, slice_width), slice_width)

    def place(block):
        return features.at[pl.ds(pl.multiple_of(block * rows, rows), rows), columns]

    pending = []

    def send(source, block, send_sem, recv_sem, peer):
        copy = pltpu.make_async_remote_copy(
            src_ref=source,
            dst_ref=place(block),
            send_sem=send_sem,
            recv_sem=recv_sem,
            device_id=peer,
            device_id_type=MESH,
        )
        copy.start()
        pending.append(copy)

    def arrive(block):
        pltpu.make_async_remote_copy(
            src_ref=place(block),
            dst_ref=place(block),
            send_sem=line_send.at[0],
            recv_sem=ctx_recv.at[block],
            device_id=(ctx, cand),
            device_id_type=MESH,
        ).wait_recv()

    def share(source, block, slot):
        for step, peer in enumerate(cand_peers):
            send(
                source, block, cand_send.at[slot, step], cand_recv.at[block, step], (ctx, peer)
            )

    for step, peer in enumerate(line_peers):
        send(history, ctx, line_send.at[step], ctx_recv.at[ctx], (peer, cand))
    send(history, ctx, first_send.at[0], ctx_recv.at[ctx], (first, cand))
    send(history, ctx, second_send.at[0], ctx_recv.at[ctx], (second, cand))
    share(history, ctx, 0)
    own_user = pl.ds(pl.multiple_of(cand * user_rows, user_rows), user_rows)
    for step, peer in enumerate(cand_peers):
        copy = pltpu.make_async_remote_copy(
            src_ref=user,
            dst_ref=user_full.at[own_user],
            send_sem=user_send.at[step],
            recv_sem=user_recv.at[step],
            device_id=(ctx, peer),
            device_id_type=MESH,
        )
        copy.start()
        pending.append(copy)
    user_full[own_user, :] = user[...]
    features[pl.ds(pl.multiple_of(ctx * rows, rows), rows), columns] = history[...]

    for step in range(depth):
        if step > 0:
            block = flip(line, step) * 4 + low
            arrive(block)
            send(place(block), block, first_send.at[step], ctx_recv.at[block], (first, cand))
            send(place(block), block, second_send.at[step], ctx_recv.at[block], (second, cand))
            share(place(block), block, step)
        block = flip(line, step) * 4 + first % 4
        arrive(block)
        send(place(block), block, second_send.at[depth + step], ctx_recv.at[block], (second, cand))
        share(place(block), block, depth + step)
    for step in range(depth):
        for part, corner in enumerate((second % 4, 3 - low)):
            block = flip(line, step) * 4 + corner
            arrive(block)
            share(place(block), block, (2 + part) * depth + step)
    for step in range(1, cand_count):
        source = (cand + cand_count - step) % cand_count
        there = pl.ds(pl.multiple_of(source * slice_width, slice_width), slice_width)
        user_there = pl.ds(pl.multiple_of(source * user_rows, user_rows), user_rows)
        for block in range(ctx_count):
            landed = features.at[pl.ds(block * rows, rows), there]
            pltpu.make_async_remote_copy(
                src_ref=landed,
                dst_ref=landed,
                send_sem=cand_send.at[0, 0],
                recv_sem=cand_recv.at[block, step - 1],
                device_id=(ctx, cand),
                device_id_type=MESH,
            ).wait_recv()
        pltpu.make_async_remote_copy(
            src_ref=user_full.at[user_there],
            dst_ref=user_full.at[user_there],
            send_sem=user_send.at[0],
            recv_sem=user_recv.at[step - 1],
            device_id=(ctx, cand),
            device_id_type=MESH,
        ).wait_recv()
    for copy in pending:
        copy.wait_send()


def gather_history(history, user_weights):
    ctx_count, cand_count = lax.axis_size("ctx"), lax.axis_size("cand")
    rows, slice_width = history.shape
    user_rows, hidden = user_weights.shape
    depth = ctx_count // 4
    others = cand_count - 1
    return pl.pallas_call(
        functools.partial(history_kernel, ctx_count, cand_count),
        out_shape=(
            jax.ShapeDtypeStruct((rows * ctx_count, slice_width * cand_count), history.dtype),
            jax.ShapeDtypeStruct((user_rows * cand_count, hidden), user_weights.dtype),
        ),
        in_specs=[VMEM, VMEM],
        out_specs=(VMEM, VMEM),
        scratch_shapes=[
            DMA((max(depth - 1, 1),)),
            DMA((depth,)),
            DMA((2 * depth,)),
            DMA((ctx_count, others)),
            DMA((ctx_count,)),
            DMA((ctx_count, others)),
            DMA((others,)),
            DMA((others,)),
        ],
        compiler_params=kernel_params(0),
        name="history_gather",
    )(history, user_weights)


def swap_cores(cand_count, source, slots, send_sem, recv_sem):
    ctx = lax.axis_index("ctx")
    cand = lax.axis_index("cand")
    copies = []
    for step in range(1, cand_count):
        copy = pltpu.make_async_remote_copy(
            src_ref=source,
            dst_ref=slots.at[step - 1],
            send_sem=send_sem.at[step - 1],
            recv_sem=recv_sem.at[step - 1],
            device_id=(ctx, (cand + step) % cand_count),
            device_id_type=MESH,
        )
        copy.start()
        copies.append(copy)
    return copies


def ordered_sum(cand_count, own, slots):
    cand = lax.axis_index("cand")
    total = None
    for owner in range(cand_count):
        term = own[...]
        for step in range(1, cand_count):
            term = jnp.where((owner + step) % cand_count == cand, slots[step - 1], term)
        total = term if total is None else total + term
    return total


def user_grad_kernel(
    ctx_count, cand_count, part, out, slots, core_send, core_recv, send_sem, recv_sem
):
    ctx = lax.axis_index("ctx")
    cand = lax.axis_index("cand")
    ctx_peers = [(ctx + step) % ctx_count for step in range(1, ctx_count)]
    meet(
        [(ctx, (cand + step) % cand_count) for step in range(1, cand_count)]
        + [(peer, cand) for peer in ctx_peers]
    )
    copies = swap_cores(cand_count, part, slots, core_send, core_recv)
    for copy in copies:
        copy.wait()
    out[ctx] = ordered_sum(cand_count, part, slots)
    copies = []
    for step, peer in enumerate(ctx_peers):
        copy = pltpu.make_async_remote_copy(
            src_ref=out.at[ctx],
            dst_ref=out.at[ctx],
            send_sem=send_sem.at[step],
            recv_sem=recv_sem.at[step],
            device_id=(peer, cand),
            device_id_type=MESH,
        )
        copy.start()
        copies.append(copy)
    for step, copy in enumerate(copies):
        source = (ctx + ctx_count - step - 1) % ctx_count
        pltpu.make_async_remote_copy(
            src_ref=out.at[source],
            dst_ref=out.at[source],
            send_sem=send_sem.at[step],
            recv_sem=recv_sem.at[step],
            device_id=(ctx, cand),
            device_id_type=MESH,
        ).wait_recv()
    for copy in copies:
        copy.wait_send()


def gather_user_grad(part):
    ctx_count, cand_count = lax.axis_size("ctx"), lax.axis_size("cand")
    others = cand_count - 1
    gathered = pl.pallas_call(
        functools.partial(user_grad_kernel, ctx_count, cand_count),
        out_shape=jax.ShapeDtypeStruct((ctx_count,) + part.shape, F32),
        in_specs=[VMEM],
        out_specs=VMEM,
        scratch_shapes=[
            pltpu.VMEM((others,) + part.shape, F32),
            DMA((others,)),
            DMA((others,)),
            DMA((ctx_count - 1,)),
            DMA((ctx_count - 1,)),
        ],
        compiler_params=kernel_params(1),
        name="user_grad_gather",
    )(part)
    return gathered.reshape(ctx_count * part.shape[0], part.shape[1])


def core_sum_kernel(cand_count, part, out, slots, send_sem, recv_sem):
    ctx = lax.axis_index("ctx")
    cand = lax.axis_index("cand")
    meet([(ctx, (cand + step) % cand_count) for step in range(1, cand_count)])
    for copy in swap_cores(cand_count, part, slots, send_sem, recv_sem):
        copy.wait()
    out[...] = ordered_sum(cand_count, part, slots)


def core_sum(part, collective_id):
    cand_count = lax.axis_size("cand")
    others = cand_count - 1
    return pl.pallas_call(
        functools.partial(core_sum_kernel, cand_count),
        out_shape=jax.ShapeDtypeStruct(part.shape, F32),
        in_specs=[VMEM],
        out_specs=VMEM,
        scratch_shapes=[
            pltpu.VMEM((others,) + part.shape, F32),
            DMA((others,)),
            DMA((others,)),
        ],
        compiler_params=kernel_params(collective_id),
        name="core_sum",
    )(part)


def per_device(
    history,
    head_weights,
    merge_weights,
    cand_table,
    user_weights,
    item_weights,
    score_weights,
    request_points,
    candidate_owner,
    candidate_row,
    relevance,
):
    row_count, slice_width = history.shape
    width = head_weights.shape[0]
    ctx_index = lax.axis_index("ctx")
    cand_index = lax.axis_index("cand")
    ctx_count = lax.axis_size("ctx")
    first_row = ctx_index * row_count
    heads = merge_weights.shape[0] // HEAD
    cols = heads * HEAD
    requests = request_points.shape[0]
    own_requests = candidate_row.shape[0]
    scaling = HEAD ** (-0.5)

    sections = head_weights.reshape(width, heads, 4, HEAD)
    gate_w, value_w, query_w, key_w = (
        sections[:, :, index].reshape(width, cols) for index in range(4)
    )
    item_proj = mm(cand_table, item_weights)
    features, user_full = gather_history(history, user_weights)
    length = features.shape[0]
    x_low = layer_norm(features.astype(F32))[0].astype(BF16)

    picks = (request_points[:, None] == jnp.arange(length, dtype=jnp.int32)[None, :]).astype(BF16)
    x_requests = mm(picks, x_low).astype(BF16)
    raw_requests = mm(picks, features)

    before_key = mm(x_low, key_w)
    before_value = mm(x_low, value_w)
    before_query = mm(x_requests, query_w)
    before_gate = mm(x_requests, gate_w)

    def split(array):
        return array.reshape(array.shape[0], heads, HEAD)

    key_heads = split(jax.nn.silu(before_key).astype(BF16))
    values = split(jax.nn.silu(before_value).astype(BF16))
    queries = split(jax.nn.silu(before_query).astype(BF16))
    gate_part = split(jax.nn.silu(before_gate).astype(BF16)).astype(F32)

    logits = jnp.einsum("qhd,khd->hqk", queries, key_heads, preferred_element_type=F32) * scaling
    allowed = (jnp.arange(length, dtype=jnp.int32)[None, :] <= request_points[:, None])[None]
    divisor = (request_points + 1).astype(F32)[None, :, None]
    weight = jnp.where(allowed, jax.nn.silu(logits) / divisor, 0.0).astype(BF16)
    attended = jnp.einsum("hqk,khd->qhd", weight, values, preferred_element_type=F32)
    normed, inverse = layer_norm(attended)
    gated = (normed * gate_part).astype(BF16).reshape(requests, cols)

    def own(array):
        return lax.dynamic_slice_in_dim(array, ctx_index * own_requests, own_requests, 0)

    head_total = lax.psum(mm(own(gated), merge_weights), "cand")
    layer_out = (own(raw_requests) + head_total).astype(BF16)
    user_proj = mm(layer_out, user_full)

    owned = candidate_owner == cand_index
    table_rows = jnp.arange(cand_table.shape[0], dtype=jnp.int32)
    hits = owned[:, :, None] & (candidate_row[:, :, None] == table_rows)
    pre_score = user_proj[:, None, :] + item_proj[None]
    row_scores = jnp.sum(jax.nn.silu(pre_score) * score_weights, -1)
    scores = lax.psum(jnp.sum(jnp.where(hits, row_scores[:, None, :], 0.0), -1), "cand")
    log_total = jnp.log(jnp.sum(jnp.exp(scores), -1, keepdims=True))
    target = (relevance + 1).astype(F32)
    target = target / jnp.sum(target, -1, keepdims=True)
    losses = log_total[:, 0] - jnp.sum(target * scores, -1)
    d_score = jnp.exp(scores - log_total) - target
    row_grads = jnp.sum(jnp.where(hits, d_score[:, :, None], 0.0), 1)
    user_part = jnp.sum(row_grads[:, :, None] * silu_slope(pre_score), 1) * score_weights
    d_user = gather_user_grad(user_part)

    same = request_points[:, None] == request_points[None, :]
    order = jnp.arange(requests, dtype=jnp.int32)
    earlier = jnp.any(same & (order[None, :] < order[:, None]), 1)
    merge_same = (same & ~earlier[:, None]).astype(F32)
    d_user = jnp.dot(merge_same, d_user, precision=HIGHEST)
    d_picked = jnp.dot(d_user, user_full.astype(F32).T, precision=HIGHEST)
    d_gated = split(jnp.dot(d_picked, merge_weights.astype(F32).T, precision=HIGHEST))
    d_gate = (d_gated * normed).reshape(requests, cols)
    d_attended = norm_back(d_gated * gate_part, normed, inverse).astype(BF16)

    merge_cols = width // ctx_count
    own_picked = lax.dynamic_slice_in_dim(d_picked, ctx_index * merge_cols, merge_cols, 1)
    grad_merge = lax.dot_general(
        gated.astype(F32), own_picked, (((0,), (0,)), ((), ())), precision=HIGHEST
    )

    slopes = jnp.einsum("qhd,khd->hqk", d_attended, values, preferred_element_type=F32)
    d_logit = jnp.where(allowed, slopes * silu_slope(logits) / divisor, 0.0).astype(BF16)
    d_query = jnp.einsum("hqk,khd->qhd", d_logit, key_heads, preferred_element_type=F32) * scaling
    d_key = jnp.einsum("hqk,qhd->khd", d_logit, queries, preferred_element_type=F32) * scaling
    d_value = jnp.einsum("hqk,qhd->khd", weight, d_attended, preferred_element_type=F32)

    d_before_key = (d_key.reshape(length, cols) * silu_slope(before_key)).astype(BF16)
    d_before_value = (d_value.reshape(length, cols) * silu_slope(before_value)).astype(BF16)
    d_before_query = (d_query.reshape(requests, cols) * silu_slope(before_query)).astype(BF16)
    d_before_gate = (d_gate * silu_slope(before_gate)).astype(BF16)

    def own_features(array):
        return lax.dynamic_slice_in_dim(array, ctx_index * merge_cols, merge_cols, 1)

    def grad_of(rows, grads):
        return split(lax.dot_general(rows, grads, (((0,), (0,)), ((), ())), preferred_element_type=F32))

    x_own = own_features(x_low)
    x_own_requests = own_features(x_requests)
    grad_heads = jnp.stack(
        [
            grad_of(x_own_requests, d_before_gate),
            grad_of(x_own, d_before_value),
            grad_of(x_own_requests, d_before_query),
            grad_of(x_own, d_before_key),
        ],
        2,
    ).reshape(merge_cols, 4 * cols)

    def own_rows(array):
        return lax.dynamic_slice_in_dim(array, first_row, row_count, 0)

    positions = first_row + jnp.arange(row_count, dtype=jnp.int32)
    places = positions[:, None] == request_points[None, :]
    low_places = places.astype(BF16)
    transposed = (((1,), (1,)), ((), ()))

    def back(grads, weights):
        return lax.dot_general(grads, weights, transposed, preferred_element_type=F32)

    d_normed = core_sum(
        back(own_rows(d_before_key), key_w)
        + back(own_rows(d_before_value), value_w)
        + back(mm(low_places, d_before_query).astype(BF16), query_w)
        + back(mm(low_places, d_before_gate).astype(BF16), gate_w),
        2,
    )
    x_normed, x_inverse = layer_norm(own_rows(features).astype(F32))
    column_start = cand_index * slice_width
    d_input = lax.dynamic_slice_in_dim(
        norm_back(d_normed, x_normed, x_inverse), column_start, slice_width, 1
    )
    picked_cols = lax.dynamic_slice_in_dim(d_picked, column_start, slice_width, 1)
    d_layer = jnp.dot(places.astype(F32), picked_cols, precision=HIGHEST)
    history_grad = d_layer + d_input
    return (losses, history_grad, grad_heads, grad_merge)


def solution(mesh):
    return jax.shard_map(
        per_device,
        mesh=mesh,
        in_specs=(
            P("ctx", "cand"),
            P(None, "cand"),
            P("cand", None),
            P("cand", None),
            P("cand", None),
            P(),
            P(),
            P(),
            P("ctx", None),
            P("ctx", None),
            P("ctx", None),
        ),
        out_specs=(P("ctx"), P("ctx", "cand"), P("ctx", "cand"), P("cand", "ctx")),
        check_vma=False,
    )
```

```python
import functools

import jax
import jax.numpy as jnp
from jax import lax
from jax.experimental import pallas as pl
from jax.experimental.pallas import tpu as pltpu
from jax.sharding import PartitionSpec as P

HEAD = 128
norm_eps = 1e-05
HIGHEST = lax.Precision.HIGHEST
F32 = jnp.float32
BF16 = jnp.bfloat16


def silu_slope(argument):
    sigmoid_part = jax.nn.sigmoid(argument)
    return sigmoid_part * (1.0 + argument * (1.0 - sigmoid_part))


def layer_norm(argument):
    centred = argument - jnp.mean(argument, -1, keepdims=True)
    inverse = lax.rsqrt(jnp.mean(centred * centred, -1, keepdims=True) + norm_eps)
    return (centred * inverse, inverse)


def norm_back(gradient, normed, inverse):
    return inverse * (
        gradient
        - jnp.mean(gradient, -1, keepdims=True)
        - normed * jnp.mean(gradient * normed, -1, keepdims=True)
    )


def mm(left, right):
    return jnp.dot(left, right, preferred_element_type=F32)


def back(grads, weights):
    return lax.dot_general(grads, weights, (((1,), (1,)), ((), ())), preferred_element_type=F32)


MESH = pl.DeviceIdType.MESH
VMEM = pl.BlockSpec(memory_space=pltpu.VMEM)
DMA = pltpu.SemaphoreType.DMA


def kernel_params(collective_id):
    return pltpu.CompilerParams(
        collective_id=collective_id, has_side_effects=True, vmem_limit_bytes=60 * 1024 * 1024
    )


def flip(number, bits):
    place = 1
    result = number
    while place <= bits:
        if bits & place:
            result = result + place - 2 * place * ((number // place) % 2)
        place *= 2
    return result


def meet(peers):
    barrier = pltpu.get_barrier_semaphore()
    for peer in peers:
        pl.semaphore_signal(barrier, inc=1, device_id=peer, device_id_type=MESH)
    pl.semaphore_wait(barrier, len(peers))


def history_kernel(
    ctx_count,
    cand_count,
    heads,
    history,
    user,
    points,
    head_weights,
    cand_table,
    item_weights,
    x_low,
    before_key,
    before_value,
    key_heads,
    values,
    x_requests,
    raw_requests,
    before_query,
    before_gate,
    attended,
    x_own,
    x_inverse,
    user_full,
    item_proj,
    features,
    weights,
    table,
    item,
    x_sum,
    raw_sum,
    weight_sem,
    item_sem,
    line_send,
    first_send,
    second_send,
    cand_send,
    ctx_recv,
    cand_recv,
    user_send,
    user_recv,
):
    rows, slice_width = history.shape
    user_rows = user.shape[0]
    ctx = lax.axis_index("ctx")
    cand = lax.axis_index("cand")
    depth = ctx_count // 4
    line, low = ctx // 4, ctx % 4
    odd = cand % 2
    flip_x, flip_y = flip(ctx, 1), flip(ctx, 2)
    first = flip_x + odd * (flip_y - flip_x)
    second = flip_y + odd * (flip_x - flip_y)
    line_peers = [flip(line, step) * 4 + low for step in range(1, depth)]
    cand_peers = [(cand + step) % cand_count for step in range(1, cand_count)]
    meet(
        [(peer, cand) for peer in line_peers]
        + [(first, cand), (second, cand)]
        + [(ctx, peer) for peer in cand_peers]
    )
    columns = pl.ds(pl.multiple_of(cand * slice_width, slice_width), slice_width)

    def place(block):
        return features.at[pl.ds(pl.multiple_of(block * rows, rows), rows), columns]

    pending = []

    def send(source, block, send_sem, recv_sem, peer):
        copy = pltpu.make_async_remote_copy(
            src_ref=source,
            dst_ref=place(block),
            send_sem=send_sem,
            recv_sem=recv_sem,
            device_id=peer,
            device_id_type=MESH,
        )
        copy.start()
        pending.append(copy)

    def arrive(block):
        pltpu.make_async_remote_copy(
            src_ref=place(block),
            dst_ref=place(block),
            send_sem=line_send.at[0],
            recv_sem=ctx_recv.at[block],
            device_id=(ctx, cand),
            device_id_type=MESH,
        ).wait_recv()

    def share(source, block, slot):
        for step, peer in enumerate(cand_peers):
            send(
                source, block, cand_send.at[slot, step], cand_recv.at[block, step], (ctx, peer)
            )

    for step, peer in enumerate(line_peers):
        send(history, ctx, line_send.at[step], ctx_recv.at[ctx], (peer, cand))
    send(history, ctx, first_send.at[0], ctx_recv.at[ctx], (first, cand))
    send(history, ctx, second_send.at[0], ctx_recv.at[ctx], (second, cand))
    share(history, ctx, 0)
    own_user = pl.ds(pl.multiple_of(cand * user_rows, user_rows), user_rows)
    for step, peer in enumerate(cand_peers):
        copy = pltpu.make_async_remote_copy(
            src_ref=user,
            dst_ref=user_full.at[own_user],
            send_sem=user_send.at[step],
            recv_sem=user_recv.at[step],
            device_id=(ctx, peer),
            device_id_type=MESH,
        )
        copy.start()
        pending.append(copy)
    weight_copies = []
    for head in range(heads):
        for section in range(4):
            copy = pltpu.make_async_copy(
                head_weights.at[:, pl.ds((4 * head + section) * HEAD, HEAD)],
                weights.at[section, :, pl.ds(head * HEAD, HEAD)],
                weight_sem.at[4 * head + section],
            )
            copy.start()
            weight_copies.append(copy)
    item_copies = [
        pltpu.make_async_copy(cand_table, table, item_sem.at[0]),
        pltpu.make_async_copy(item_weights, item, item_sem.at[1]),
    ]
    for copy in item_copies:
        copy.start()
    user_full[own_user, :] = user[...]
    features[pl.ds(pl.multiple_of(ctx * rows, rows), rows), columns] = history[...]

    x_sum[...] = jnp.zeros_like(x_sum)
    raw_sum[...] = jnp.zeros_like(raw_sum)
    requests = points.shape[0]

    def project(block):
        for step in range(1, cand_count):
            source = (cand + cand_count - step) % cand_count
            there = pl.ds(pl.multiple_of(source * slice_width, slice_width), slice_width)
            landed = features.at[pl.ds(pl.multiple_of(block * rows, rows), rows), there]
            pltpu.make_async_remote_copy(
                src_ref=landed,
                dst_ref=landed,
                send_sem=cand_send.at[0, 0],
                recv_sem=cand_recv.at[block, step - 1],
                device_id=(ctx, cand),
                device_id_type=MESH,
            ).wait_recv()
        span = pl.ds(pl.multiple_of(block * rows, rows), rows)
        raw = features[span, :]
        normed, inverse = layer_norm(raw.astype(F32))
        low_block = normed.astype(BF16)
        x_low[span, :] = low_block
        position = block * rows + lax.broadcasted_iota(jnp.int32, (requests, rows), 1)
        picks = jnp.where(points[...] == position, 1.0, 0.0).astype(BF16)
        x_sum[...] += mm(picks, low_block)
        raw_sum[...] += mm(picks, raw)
        key_part = mm(low_block, weights[3])
        before_key[span, :] = key_part
        key_heads[span, :] = (key_part * jax.nn.sigmoid(key_part)).astype(BF16)
        value_part = mm(low_block, weights[1])
        before_value[span, :] = value_part
        values[span, :] = (value_part * jax.nn.sigmoid(value_part)).astype(BF16)
        return normed, inverse

    for copy in item_copies:
        copy.wait()
    item_proj[...] = mm(table[...], item[...])
    for copy in weight_copies:
        copy.wait()

    for step in range(depth):
        line_block = flip(line, step) * 4 + low
        if step > 0:
            block = line_block
            arrive(block)
            send(place(block), block, first_send.at[step], ctx_recv.at[block], (first, cand))
            send(place(block), block, second_send.at[step], ctx_recv.at[block], (second, cand))
            share(place(block), block, step)
        block = flip(line, step) * 4 + first % 4
        arrive(block)
        send(place(block), block, second_send.at[depth + step], ctx_recv.at[block], (second, cand))
        share(place(block), block, depth + step)
        normed, inverse = project(line_block)
        if step == 0:
            x_own[...] = normed
            x_inverse[...] = inverse
    for step in range(depth):
        lines = flip(line, step) * 4
        for part, corner in enumerate((second % 4, 3 - low)):
            block = lines + corner
            arrive(block)
            share(place(block), block, (2 + part) * depth + step)
            project(lines + (first % 4, second % 4)[part])
        if step > 0:
            project(flip(line, step - 1) * 4 + 3 - low)
    project(flip(line, depth - 1) * 4 + 3 - low)

    x_request = x_sum[...].astype(BF16)
    x_requests[...] = x_request
    raw_requests[...] = raw_sum[...]
    query_part = mm(x_request, weights[2])
    before_query[...] = query_part
    before_gate[...] = mm(x_request, weights[0])
    queries = (query_part * jax.nn.sigmoid(query_part)).astype(BF16)
    divisor = (points[...] + 1).astype(F32)
    chunk = 4 * rows
    for head in range(heads):
        span = pl.ds(head * HEAD, HEAD)
        query = queries[:, head * HEAD : (head + 1) * HEAD]

        def add_chunk(index, total):
            start = pl.multiple_of(index * chunk, chunk)
            logits = back(query, key_heads[pl.ds(start, chunk), span]) * HEAD ** (-0.5)
            position = start + lax.broadcasted_iota(jnp.int32, (requests, chunk), 1)
            weight = jnp.where(
                position <= points[...], logits * jax.nn.sigmoid(logits) / divisor, 0.0
            ).astype(BF16)
            return total + mm(weight, values[pl.ds(start, chunk), span])

        attended[:, span] = lax.fori_loop(
            0, ctx_count * rows // chunk, add_chunk, jnp.zeros((requests, HEAD), F32)
        )

    for step in range(1, cand_count):
        source = (cand + cand_count - step) % cand_count
        user_there = pl.ds(pl.multiple_of(source * user_rows, user_rows), user_rows)
        pltpu.make_async_remote_copy(
            src_ref=user_full.at[user_there],
            dst_ref=user_full.at[user_there],
            send_sem=user_send.at[0],
            recv_sem=user_recv.at[step - 1],
            device_id=(ctx, cand),
            device_id_type=MESH,
        ).wait_recv()
    for copy in pending:
        copy.wait_send()


def gather_history(history, user_weights, points, head_weights, cand_table, item_weights):
    ctx_count, cand_count = lax.axis_size("ctx"), lax.axis_size("cand")
    rows, slice_width = history.shape
    user_rows, hidden = user_weights.shape
    requests = points.shape[0]
    width = head_weights.shape[0]
    length = rows * ctx_count
    cols = head_weights.shape[1] // 4
    heads = cols // HEAD
    depth = ctx_count // 4
    others = cand_count - 1
    shape = jax.ShapeDtypeStruct
    outputs = (
        shape((length, width), BF16),
        shape((length, cols), F32),
        shape((length, cols), F32),
        shape((length, cols), BF16),
        shape((length, cols), BF16),
        shape((requests, width), BF16),
        shape((requests, width), F32),
        shape((requests, cols), F32),
        shape((requests, cols), F32),
        shape((requests, cols), F32),
        shape((rows, width), F32),
        shape((rows, 1), F32),
        shape((user_rows * cand_count, hidden), BF16),
        shape((cand_table.shape[0], hidden), F32),
    )
    anywhere = pl.BlockSpec(memory_space=pl.ANY)
    return pl.pallas_call(
        functools.partial(history_kernel, ctx_count, cand_count, heads),
        out_shape=outputs,
        in_specs=[VMEM] * 3 + [anywhere] * 3,
        out_specs=(VMEM,) * len(outputs),
        scratch_shapes=[
            pltpu.VMEM((length, width), BF16),
            pltpu.VMEM((4, width, cols), BF16),
            pltpu.VMEM(cand_table.shape, BF16),
            pltpu.VMEM(item_weights.shape, BF16),
            pltpu.VMEM((requests, width), F32),
            pltpu.VMEM((requests, width), F32),
            DMA((4 * heads,)),
            DMA((2,)),
            DMA((max(depth - 1, 1),)),
            DMA((depth,)),
            DMA((2 * depth,)),
            DMA((ctx_count, others)),
            DMA((ctx_count,)),
            DMA((ctx_count, others)),
            DMA((others,)),
            DMA((others,)),
        ],
        compiler_params=kernel_params(0),
        name="history_project",
    )(history, user_weights, points, head_weights, cand_table, item_weights)


def swap_cores(cand_count, source, slots, send_sem, recv_sem):
    ctx = lax.axis_index("ctx")
    cand = lax.axis_index("cand")
    copies = []
    for step in range(1, cand_count):
        copy = pltpu.make_async_remote_copy(
            src_ref=source,
            dst_ref=slots.at[step - 1],
            send_sem=send_sem.at[step - 1],
            recv_sem=recv_sem.at[step - 1],
            device_id=(ctx, (cand + step) % cand_count),
            device_id_type=MESH,
        )
        copy.start()
        copies.append(copy)
    return copies


def ordered_sum(cand_count, own, slots):
    cand = lax.axis_index("cand")
    total = None
    for owner in range(cand_count):
        term = own[...]
        for step in range(1, cand_count):
            term = jnp.where((owner + step) % cand_count == cand, slots[step - 1], term)
        total = term if total is None else total + term
    return total


def user_grad_kernel(
    ctx_count, cand_count, part, out, slots, core_send, core_recv, send_sem, recv_sem
):
    ctx = lax.axis_index("ctx")
    cand = lax.axis_index("cand")
    ctx_peers = [(ctx + step) % ctx_count for step in range(1, ctx_count)]
    meet(
        [(ctx, (cand + step) % cand_count) for step in range(1, cand_count)]
        + [(peer, cand) for peer in ctx_peers]
    )
    copies = swap_cores(cand_count, part, slots, core_send, core_recv)
    for copy in copies:
        copy.wait()
    out[ctx] = ordered_sum(cand_count, part, slots)
    copies = []
    for step, peer in enumerate(ctx_peers):
        copy = pltpu.make_async_remote_copy(
            src_ref=out.at[ctx],
            dst_ref=out.at[ctx],
            send_sem=send_sem.at[step],
            recv_sem=recv_sem.at[step],
            device_id=(peer, cand),
            device_id_type=MESH,
        )
        copy.start()
        copies.append(copy)
    for step, copy in enumerate(copies):
        source = (ctx + ctx_count - step - 1) % ctx_count
        pltpu.make_async_remote_copy(
            src_ref=out.at[source],
            dst_ref=out.at[source],
            send_sem=send_sem.at[step],
            recv_sem=recv_sem.at[step],
            device_id=(ctx, cand),
            device_id_type=MESH,
        ).wait_recv()
    for copy in copies:
        copy.wait_send()


def gather_user_grad(part):
    ctx_count, cand_count = lax.axis_size("ctx"), lax.axis_size("cand")
    others = cand_count - 1
    gathered = pl.pallas_call(
        functools.partial(user_grad_kernel, ctx_count, cand_count),
        out_shape=jax.ShapeDtypeStruct((ctx_count,) + part.shape, F32),
        in_specs=[VMEM],
        out_specs=VMEM,
        scratch_shapes=[
            pltpu.VMEM((others,) + part.shape, F32),
            DMA((others,)),
            DMA((others,)),
            DMA((ctx_count - 1,)),
            DMA((ctx_count - 1,)),
        ],
        compiler_params=kernel_params(1),
        name="user_grad_gather",
    )(part)
    return gathered.reshape(ctx_count * part.shape[0], part.shape[1])


def core_sum_kernel(cand_count, part, out, slots, send_sem, recv_sem):
    ctx = lax.axis_index("ctx")
    cand = lax.axis_index("cand")
    meet([(ctx, (cand + step) % cand_count) for step in range(1, cand_count)])
    for copy in swap_cores(cand_count, part, slots, send_sem, recv_sem):
        copy.wait()
    out[...] = ordered_sum(cand_count, part, slots)


def core_sum(part, collective_id):
    cand_count = lax.axis_size("cand")
    others = cand_count - 1
    return pl.pallas_call(
        functools.partial(core_sum_kernel, cand_count),
        out_shape=jax.ShapeDtypeStruct(part.shape, F32),
        in_specs=[VMEM],
        out_specs=VMEM,
        scratch_shapes=[
            pltpu.VMEM((others,) + part.shape, F32),
            DMA((others,)),
            DMA((others,)),
        ],
        compiler_params=kernel_params(collective_id),
        name="core_sum",
    )(part)


def per_device(
    history,
    head_weights,
    merge_weights,
    cand_table,
    user_weights,
    item_weights,
    score_weights,
    request_points,
    candidate_owner,
    candidate_row,
    relevance,
):
    row_count, slice_width = history.shape
    width = head_weights.shape[0]
    ctx_index = lax.axis_index("ctx")
    cand_index = lax.axis_index("cand")
    ctx_count = lax.axis_size("ctx")
    first_row = ctx_index * row_count
    heads = merge_weights.shape[0] // HEAD
    cols = heads * HEAD
    requests = request_points.shape[0]
    own_requests = candidate_row.shape[0]
    scaling = HEAD ** (-0.5)

    sections = head_weights.reshape(width, heads, 4, HEAD)
    gate_w, value_w, query_w, key_w = (
        sections[:, :, index].reshape(width, cols) for index in range(4)
    )
    (
        x_low,
        before_key,
        before_value,
        key_heads,
        values,
        x_requests,
        raw_requests,
        before_query,
        before_gate,
        attended,
        x_normed,
        x_inverse,
        user_full,
        item_proj,
    ) = gather_history(
        history, user_weights, request_points[:, None], head_weights, cand_table, item_weights
    )
    length = x_low.shape[0]

    def split(array):
        return array.reshape(array.shape[0], heads, HEAD)

    key_heads = split(key_heads)
    values = split(values)
    queries = split(jax.nn.silu(before_query).astype(BF16))
    gate_part = split(jax.nn.silu(before_gate).astype(BF16)).astype(F32)

    logits = jnp.einsum("qhd,khd->hqk", queries, key_heads, preferred_element_type=F32) * scaling
    allowed = (jnp.arange(length, dtype=jnp.int32)[None, :] <= request_points[:, None])[None]
    divisor = (request_points + 1).astype(F32)[None, :, None]
    weight = jnp.where(allowed, jax.nn.silu(logits) / divisor, 0.0).astype(BF16)
    normed, inverse = layer_norm(split(attended))
    gated = (normed * gate_part).astype(BF16).reshape(requests, cols)

    def own(array):
        return lax.dynamic_slice_in_dim(array, ctx_index * own_requests, own_requests, 0)

    head_total = lax.psum(mm(own(gated), merge_weights), "cand")
    layer_out = (own(raw_requests) + head_total).astype(BF16)
    user_proj = mm(layer_out, user_full)

    owned = candidate_owner == cand_index
    table_rows = jnp.arange(cand_table.shape[0], dtype=jnp.int32)
    hits = owned[:, :, None] & (candidate_row[:, :, None] == table_rows)
    pre_score = user_proj[:, None, :] + item_proj[None]
    row_scores = jnp.sum(jax.nn.silu(pre_score) * score_weights, -1)
    scores = lax.psum(jnp.sum(jnp.where(hits, row_scores[:, None, :], 0.0), -1), "cand")
    log_total = jnp.log(jnp.sum(jnp.exp(scores), -1, keepdims=True))
    target = (relevance + 1).astype(F32)
    target = target / jnp.sum(target, -1, keepdims=True)
    losses = log_total[:, 0] - jnp.sum(target * scores, -1)
    d_score = jnp.exp(scores - log_total) - target
    row_grads = jnp.sum(jnp.where(hits, d_score[:, :, None], 0.0), 1)
    user_part = jnp.sum(row_grads[:, :, None] * silu_slope(pre_score), 1) * score_weights
    d_user = gather_user_grad(user_part)

    same = request_points[:, None] == request_points[None, :]
    order = jnp.arange(requests, dtype=jnp.int32)
    earlier = jnp.any(same & (order[None, :] < order[:, None]), 1)
    merge_same = (same & ~earlier[:, None]).astype(F32)
    d_user = jnp.dot(merge_same, d_user, precision=HIGHEST)
    d_picked = jnp.dot(d_user, user_full.astype(F32).T, precision=HIGHEST)
    d_gated = split(jnp.dot(d_picked, merge_weights.astype(F32).T, precision=HIGHEST))
    d_gate = (d_gated * normed).reshape(requests, cols)
    d_attended = norm_back(d_gated * gate_part, normed, inverse).astype(BF16)

    merge_cols = width // ctx_count
    own_picked = lax.dynamic_slice_in_dim(d_picked, ctx_index * merge_cols, merge_cols, 1)
    grad_merge = lax.dot_general(
        gated.astype(F32), own_picked, (((0,), (0,)), ((), ())), precision=HIGHEST
    )

    slopes = jnp.einsum("qhd,khd->hqk", d_attended, values, preferred_element_type=F32)
    d_logit = jnp.where(allowed, slopes * silu_slope(logits) / divisor, 0.0).astype(BF16)
    d_query = jnp.einsum("hqk,khd->qhd", d_logit, key_heads, preferred_element_type=F32) * scaling
    d_key = jnp.einsum("hqk,qhd->khd", d_logit, queries, preferred_element_type=F32) * scaling
    d_value = jnp.einsum("hqk,qhd->khd", weight, d_attended, preferred_element_type=F32)

    d_before_key = (d_key.reshape(length, cols) * silu_slope(before_key)).astype(BF16)
    d_before_value = (d_value.reshape(length, cols) * silu_slope(before_value)).astype(BF16)
    d_before_query = (d_query.reshape(requests, cols) * silu_slope(before_query)).astype(BF16)
    d_before_gate = (d_gate * silu_slope(before_gate)).astype(BF16)

    def own_features(array):
        return lax.dynamic_slice_in_dim(array, ctx_index * merge_cols, merge_cols, 1)

    def grad_of(rows, grads):
        return split(lax.dot_general(rows, grads, (((0,), (0,)), ((), ())), preferred_element_type=F32))

    x_own = own_features(x_low)
    x_own_requests = own_features(x_requests)
    grad_heads = jnp.stack(
        [
            grad_of(x_own_requests, d_before_gate),
            grad_of(x_own, d_before_value),
            grad_of(x_own_requests, d_before_query),
            grad_of(x_own, d_before_key),
        ],
        2,
    ).reshape(merge_cols, 4 * cols)

    def own_rows(array):
        return lax.dynamic_slice_in_dim(array, first_row, row_count, 0)

    positions = first_row + jnp.arange(row_count, dtype=jnp.int32)
    places = positions[:, None] == request_points[None, :]
    low_places = places.astype(BF16)
    d_normed = core_sum(
        back(own_rows(d_before_key), key_w)
        + back(own_rows(d_before_value), value_w)
        + back(mm(low_places, d_before_query).astype(BF16), query_w)
        + back(mm(low_places, d_before_gate).astype(BF16), gate_w),
        2,
    )
    column_start = cand_index * slice_width
    d_input = lax.dynamic_slice_in_dim(
        norm_back(d_normed, x_normed, x_inverse), column_start, slice_width, 1
    )
    picked_cols = lax.dynamic_slice_in_dim(d_picked, column_start, slice_width, 1)
    d_layer = jnp.dot(places.astype(F32), picked_cols, precision=HIGHEST)
    history_grad = d_layer + d_input
    return (losses, history_grad, grad_heads, grad_merge)


def solution(mesh):
    return jax.shard_map(
        per_device,
        mesh=mesh,
        in_specs=(
            P("ctx", "cand"),
            P(None, "cand"),
            P("cand", None),
            P("cand", None),
            P("cand", None),
            P(),
            P(),
            P(),
            P("ctx", None),
            P("ctx", None),
            P("ctx", None),
        ),
        out_specs=(P("ctx"), P("ctx", "cand"), P("ctx", "cand"), P("cand", "ctx")),
        check_vma=False,
    )
```

```python
import functools

import jax
import jax.numpy as jnp
from jax import lax
from jax.experimental import pallas as pl
from jax.experimental.pallas import tpu as pltpu
from jax.sharding import PartitionSpec as P

HEAD = 128
norm_eps = 1e-05
HIGHEST = lax.Precision.HIGHEST
F32 = jnp.float32
BF16 = jnp.bfloat16


def silu_slope(argument):
    sigmoid_part = jax.nn.sigmoid(argument)
    return sigmoid_part * (1.0 + argument * (1.0 - sigmoid_part))


def layer_norm(argument):
    centred = argument - jnp.mean(argument, -1, keepdims=True)
    inverse = lax.rsqrt(jnp.mean(centred * centred, -1, keepdims=True) + norm_eps)
    return (centred * inverse, inverse)


def norm_back(gradient, normed, inverse):
    return inverse * (
        gradient
        - jnp.mean(gradient, -1, keepdims=True)
        - normed * jnp.mean(gradient * normed, -1, keepdims=True)
    )


def mm(left, right):
    return jnp.dot(left, right, preferred_element_type=F32)


def back(grads, weights):
    return lax.dot_general(grads, weights, (((1,), (1,)), ((), ())), preferred_element_type=F32)


MESH = pl.DeviceIdType.MESH
VMEM = pl.BlockSpec(memory_space=pltpu.VMEM)
DMA = pltpu.SemaphoreType.DMA


def kernel_params(collective_id):
    return pltpu.CompilerParams(
        collective_id=collective_id, has_side_effects=True, vmem_limit_bytes=60 * 1024 * 1024
    )


def flip(number, bits):
    place = 1
    result = number
    while place <= bits:
        if bits & place:
            result = result + place - 2 * place * ((number // place) % 2)
        place *= 2
    return result


def meet(peers):
    barrier = pltpu.get_barrier_semaphore()
    for peer in peers:
        pl.semaphore_signal(barrier, inc=1, device_id=peer, device_id_type=MESH)
    pl.semaphore_wait(barrier, len(peers))


def history_kernel(
    ctx_count,
    cand_count,
    heads,
    history,
    user,
    points,
    head_weights,
    cand_table,
    item_weights,
    x_low,
    before_key,
    before_value,
    key_heads,
    values,
    x_requests,
    raw_requests,
    before_query,
    before_gate,
    attended,
    x_own,
    x_inverse,
    user_full,
    item_proj,
    features,
    weights,
    table,
    item,
    x_sum,
    raw_sum,
    weight_sem,
    item_sem,
    line_send,
    first_send,
    second_send,
    cand_send,
    ctx_recv,
    cand_recv,
    user_send,
    user_recv,
):
    rows, slice_width = history.shape
    user_rows = user.shape[0]
    ctx = lax.axis_index("ctx")
    cand = lax.axis_index("cand")
    depth = ctx_count // 4
    line, low = ctx // 4, ctx % 4
    odd = cand % 2
    flip_x, flip_y = flip(ctx, 1), flip(ctx, 2)
    first = flip_x + odd * (flip_y - flip_x)
    second = flip_y + odd * (flip_x - flip_y)
    line_peers = [flip(line, step) * 4 + low for step in range(1, depth)]
    cand_peers = [(cand + step) % cand_count for step in range(1, cand_count)]
    meet(
        [(peer, cand) for peer in line_peers]
        + [(first, cand), (second, cand)]
        + [(ctx, peer) for peer in cand_peers]
    )
    columns = pl.ds(pl.multiple_of(cand * slice_width, slice_width), slice_width)

    def place(block):
        return features.at[pl.ds(pl.multiple_of(block * rows, rows), rows), columns]

    pending = []

    def send(source, block, send_sem, recv_sem, peer):
        copy = pltpu.make_async_remote_copy(
            src_ref=source,
            dst_ref=place(block),
            send_sem=send_sem,
            recv_sem=recv_sem,
            device_id=peer,
            device_id_type=MESH,
        )
        copy.start()
        pending.append(copy)

    def arrive(block):
        pltpu.make_async_remote_copy(
            src_ref=place(block),
            dst_ref=place(block),
            send_sem=line_send.at[0],
            recv_sem=ctx_recv.at[block],
            device_id=(ctx, cand),
            device_id_type=MESH,
        ).wait_recv()

    def share(source, block, slot):
        for step, peer in enumerate(cand_peers):
            send(
                source, block, cand_send.at[slot, step], cand_recv.at[block, step], (ctx, peer)
            )

    for step, peer in enumerate(line_peers):
        send(history, ctx, line_send.at[step], ctx_recv.at[ctx], (peer, cand))
    send(history, ctx, first_send.at[0], ctx_recv.at[ctx], (first, cand))
    send(history, ctx, second_send.at[0], ctx_recv.at[ctx], (second, cand))
    share(history, ctx, 0)
    own_user = pl.ds(pl.multiple_of(cand * user_rows, user_rows), user_rows)
    for step, peer in enumerate(cand_peers):
        copy = pltpu.make_async_remote_copy(
            src_ref=user,
            dst_ref=user_full.at[own_user],
            send_sem=user_send.at[step],
            recv_sem=user_recv.at[step],
            device_id=(ctx, peer),
            device_id_type=MESH,
        )
        copy.start()
        pending.append(copy)
    weight_copies = []
    for head in range(heads):
        for section in range(4):
            copy = pltpu.make_async_copy(
                head_weights.at[:, pl.ds((4 * head + section) * HEAD, HEAD)],
                weights.at[section, :, pl.ds(head * HEAD, HEAD)],
                weight_sem.at[4 * head + section],
            )
            copy.start()
            weight_copies.append(copy)
    item_copies = [
        pltpu.make_async_copy(cand_table, table, item_sem.at[0]),
        pltpu.make_async_copy(item_weights, item, item_sem.at[1]),
    ]
    for copy in item_copies:
        copy.start()
    user_full[own_user, :] = user[...]
    features[pl.ds(pl.multiple_of(ctx * rows, rows), rows), columns] = history[...]

    x_sum[...] = jnp.zeros_like(x_sum)
    raw_sum[...] = jnp.zeros_like(raw_sum)
    requests = points.shape[0]

    def project(block):
        for step in range(1, cand_count):
            source = (cand + cand_count - step) % cand_count
            there = pl.ds(pl.multiple_of(source * slice_width, slice_width), slice_width)
            landed = features.at[pl.ds(pl.multiple_of(block * rows, rows), rows), there]
            pltpu.make_async_remote_copy(
                src_ref=landed,
                dst_ref=landed,
                send_sem=cand_send.at[0, 0],
                recv_sem=cand_recv.at[block, step - 1],
                device_id=(ctx, cand),
                device_id_type=MESH,
            ).wait_recv()
        span = pl.ds(pl.multiple_of(block * rows, rows), rows)
        raw = features[span, :]
        normed, inverse = layer_norm(raw.astype(F32))
        low_block = normed.astype(BF16)
        x_low[span, :] = low_block
        position = block * rows + lax.broadcasted_iota(jnp.int32, (requests, rows), 1)
        picks = jnp.where(points[...] == position, 1.0, 0.0).astype(BF16)
        x_sum[...] += mm(picks, low_block)
        raw_sum[...] += mm(picks, raw)
        key_part = mm(low_block, weights[3])
        before_key[span, :] = key_part
        key_heads[span, :] = (key_part * jax.nn.sigmoid(key_part)).astype(BF16)
        value_part = mm(low_block, weights[1])
        before_value[span, :] = value_part
        values[span, :] = (value_part * jax.nn.sigmoid(value_part)).astype(BF16)
        return normed, inverse

    for copy in item_copies:
        copy.wait()
    item_proj[...] = mm(table[...], item[...])
    for copy in weight_copies:
        copy.wait()

    for step in range(depth):
        line_block = flip(line, step) * 4 + low
        if step > 0:
            block = line_block
            arrive(block)
            send(place(block), block, first_send.at[step], ctx_recv.at[block], (first, cand))
            send(place(block), block, second_send.at[step], ctx_recv.at[block], (second, cand))
            share(place(block), block, step)
        block = flip(line, step) * 4 + first % 4
        arrive(block)
        send(place(block), block, second_send.at[depth + step], ctx_recv.at[block], (second, cand))
        share(place(block), block, depth + step)
        normed, inverse = project(line_block)
        if step == 0:
            x_own[...] = normed
            x_inverse[...] = inverse
    for step in range(depth):
        lines = flip(line, step) * 4
        for part, corner in enumerate((second % 4, 3 - low)):
            block = lines + corner
            arrive(block)
            share(place(block), block, (2 + part) * depth + step)
            project(lines + (first % 4, second % 4)[part])
        if step > 0:
            project(flip(line, step - 1) * 4 + 3 - low)
    project(flip(line, depth - 1) * 4 + 3 - low)

    x_request = x_sum[...].astype(BF16)
    x_requests[...] = x_request
    raw_requests[...] = raw_sum[...]
    query_part = mm(x_request, weights[2])
    before_query[...] = query_part
    before_gate[...] = mm(x_request, weights[0])
    queries = (query_part * jax.nn.sigmoid(query_part)).astype(BF16)
    divisor = (points[...] + 1).astype(F32)
    chunk = 4 * rows
    for head in range(heads):
        span = pl.ds(head * HEAD, HEAD)
        query = queries[:, head * HEAD : (head + 1) * HEAD]

        def add_chunk(index, total):
            start = pl.multiple_of(index * chunk, chunk)
            logits = back(query, key_heads[pl.ds(start, chunk), span]) * HEAD ** (-0.5)
            position = start + lax.broadcasted_iota(jnp.int32, (requests, chunk), 1)
            weight = jnp.where(
                position <= points[...], logits * jax.nn.sigmoid(logits) / divisor, 0.0
            ).astype(BF16)
            return total + mm(weight, values[pl.ds(start, chunk), span])

        attended[:, span] = lax.fori_loop(
            0, ctx_count * rows // chunk, add_chunk, jnp.zeros((requests, HEAD), F32)
        )

    for step in range(1, cand_count):
        source = (cand + cand_count - step) % cand_count
        user_there = pl.ds(pl.multiple_of(source * user_rows, user_rows), user_rows)
        pltpu.make_async_remote_copy(
            src_ref=user_full.at[user_there],
            dst_ref=user_full.at[user_there],
            send_sem=user_send.at[0],
            recv_sem=user_recv.at[step - 1],
            device_id=(ctx, cand),
            device_id_type=MESH,
        ).wait_recv()
    for copy in pending:
        copy.wait_send()


def gather_history(history, user_weights, points, head_weights, cand_table, item_weights):
    ctx_count, cand_count = lax.axis_size("ctx"), lax.axis_size("cand")
    rows, slice_width = history.shape
    user_rows, hidden = user_weights.shape
    requests = points.shape[0]
    width = head_weights.shape[0]
    length = rows * ctx_count
    cols = head_weights.shape[1] // 4
    heads = cols // HEAD
    depth = ctx_count // 4
    others = cand_count - 1
    shape = jax.ShapeDtypeStruct
    outputs = (
        shape((length, width), BF16),
        shape((length, cols), F32),
        shape((length, cols), F32),
        shape((length, cols), BF16),
        shape((length, cols), BF16),
        shape((requests, width), BF16),
        shape((requests, width), F32),
        shape((requests, cols), F32),
        shape((requests, cols), F32),
        shape((requests, cols), F32),
        shape((rows, width), F32),
        shape((rows, 1), F32),
        shape((user_rows * cand_count, hidden), BF16),
        shape((cand_table.shape[0], hidden), F32),
    )
    anywhere = pl.BlockSpec(memory_space=pl.ANY)
    return pl.pallas_call(
        functools.partial(history_kernel, ctx_count, cand_count, heads),
        out_shape=outputs,
        in_specs=[VMEM] * 3 + [anywhere] * 3,
        out_specs=(VMEM,) * len(outputs),
        scratch_shapes=[
            pltpu.VMEM((length, width), BF16),
            pltpu.VMEM((4, width, cols), BF16),
            pltpu.VMEM(cand_table.shape, BF16),
            pltpu.VMEM(item_weights.shape, BF16),
            pltpu.VMEM((requests, width), F32),
            pltpu.VMEM((requests, width), F32),
            DMA((4 * heads,)),
            DMA((2,)),
            DMA((max(depth - 1, 1),)),
            DMA((depth,)),
            DMA((2 * depth,)),
            DMA((ctx_count, others)),
            DMA((ctx_count,)),
            DMA((ctx_count, others)),
            DMA((others,)),
            DMA((others,)),
        ],
        compiler_params=kernel_params(0),
        name="history_project",
    )(history, user_weights, points, head_weights, cand_table, item_weights)


def swap_cores(cand_count, source, slots, send_sem, recv_sem):
    ctx = lax.axis_index("ctx")
    cand = lax.axis_index("cand")
    copies = []
    for step in range(1, cand_count):
        copy = pltpu.make_async_remote_copy(
            src_ref=source,
            dst_ref=slots.at[step - 1],
            send_sem=send_sem.at[step - 1],
            recv_sem=recv_sem.at[step - 1],
            device_id=(ctx, (cand + step) % cand_count),
            device_id_type=MESH,
        )
        copy.start()
        copies.append(copy)
    return copies


def ordered_sum(cand_count, own, slots):
    cand = lax.axis_index("cand")
    total = None
    for owner in range(cand_count):
        term = own[...]
        for step in range(1, cand_count):
            term = jnp.where((owner + step) % cand_count == cand, slots[step - 1], term)
        total = term if total is None else total + term
    return total


def user_grad_kernel(
    ctx_count, cand_count, part, out, slots, core_send, core_recv, send_sem, recv_sem
):
    ctx = lax.axis_index("ctx")
    cand = lax.axis_index("cand")
    ctx_peers = [(ctx + step) % ctx_count for step in range(1, ctx_count)]
    meet(
        [(ctx, (cand + step) % cand_count) for step in range(1, cand_count)]
        + [(peer, cand) for peer in ctx_peers]
    )
    copies = swap_cores(cand_count, part, slots, core_send, core_recv)
    for copy in copies:
        copy.wait()
    out[ctx] = ordered_sum(cand_count, part, slots)
    copies = []
    for step, peer in enumerate(ctx_peers):
        copy = pltpu.make_async_remote_copy(
            src_ref=out.at[ctx],
            dst_ref=out.at[ctx],
            send_sem=send_sem.at[step],
            recv_sem=recv_sem.at[step],
            device_id=(peer, cand),
            device_id_type=MESH,
        )
        copy.start()
        copies.append(copy)
    for step, copy in enumerate(copies):
        source = (ctx + ctx_count - step - 1) % ctx_count
        pltpu.make_async_remote_copy(
            src_ref=out.at[source],
            dst_ref=out.at[source],
            send_sem=send_sem.at[step],
            recv_sem=recv_sem.at[step],
            device_id=(ctx, cand),
            device_id_type=MESH,
        ).wait_recv()
    for copy in copies:
        copy.wait_send()


def gather_user_grad(part):
    ctx_count, cand_count = lax.axis_size("ctx"), lax.axis_size("cand")
    others = cand_count - 1
    gathered = pl.pallas_call(
        functools.partial(user_grad_kernel, ctx_count, cand_count),
        out_shape=jax.ShapeDtypeStruct((ctx_count,) + part.shape, F32),
        in_specs=[VMEM],
        out_specs=VMEM,
        scratch_shapes=[
            pltpu.VMEM((others,) + part.shape, F32),
            DMA((others,)),
            DMA((others,)),
            DMA((ctx_count - 1,)),
            DMA((ctx_count - 1,)),
        ],
        compiler_params=kernel_params(1),
        name="user_grad_gather",
    )(part)
    return gathered.reshape(ctx_count * part.shape[0], part.shape[1])


def core_sum_kernel(cand_count, part, out, slots, send_sem, recv_sem):
    ctx = lax.axis_index("ctx")
    cand = lax.axis_index("cand")
    meet([(ctx, (cand + step) % cand_count) for step in range(1, cand_count)])
    for copy in swap_cores(cand_count, part, slots, send_sem, recv_sem):
        copy.wait()
    out[...] = ordered_sum(cand_count, part, slots)


def core_sum(part, collective_id):
    cand_count = lax.axis_size("cand")
    others = cand_count - 1
    return pl.pallas_call(
        functools.partial(core_sum_kernel, cand_count),
        out_shape=jax.ShapeDtypeStruct(part.shape, F32),
        in_specs=[VMEM],
        out_specs=VMEM,
        scratch_shapes=[
            pltpu.VMEM((others,) + part.shape, F32),
            DMA((others,)),
            DMA((others,)),
        ],
        compiler_params=kernel_params(collective_id),
        name="core_sum",
    )(part)


def per_device(
    history,
    head_weights,
    merge_weights,
    cand_table,
    user_weights,
    item_weights,
    score_weights,
    request_points,
    candidate_owner,
    candidate_row,
    relevance,
):
    row_count, slice_width = history.shape
    width = head_weights.shape[0]
    ctx_index = lax.axis_index("ctx")
    cand_index = lax.axis_index("cand")
    ctx_count = lax.axis_size("ctx")
    first_row = ctx_index * row_count
    heads = merge_weights.shape[0] // HEAD
    cols = heads * HEAD
    requests = request_points.shape[0]
    own_requests = candidate_row.shape[0]
    scaling = HEAD ** (-0.5)

    (
        x_low,
        before_key,
        before_value,
        key_heads,
        values,
        x_requests,
        raw_requests,
        before_query,
        before_gate,
        attended,
        x_normed,
        x_inverse,
        user_full,
        item_proj,
    ) = gather_history(
        history, user_weights, request_points[:, None], head_weights, cand_table, item_weights
    )
    length = x_low.shape[0]

    def split(array):
        return array.reshape(array.shape[0], heads, HEAD)

    key_heads = split(key_heads)
    values = split(values)
    queries = split(jax.nn.silu(before_query).astype(BF16))
    gate_part = split(jax.nn.silu(before_gate).astype(BF16)).astype(F32)

    logits = jnp.einsum("qhd,khd->hqk", queries, key_heads, preferred_element_type=F32) * scaling
    allowed = (jnp.arange(length, dtype=jnp.int32)[None, :] <= request_points[:, None])[None]
    divisor = (request_points + 1).astype(F32)[None, :, None]
    weight = jnp.where(allowed, jax.nn.silu(logits) / divisor, 0.0).astype(BF16)
    normed, inverse = layer_norm(split(attended))
    gated = (normed * gate_part).astype(BF16).reshape(requests, cols)

    def own(array):
        return lax.dynamic_slice_in_dim(array, ctx_index * own_requests, own_requests, 0)

    head_total = lax.psum(mm(own(gated), merge_weights), "cand")
    layer_out = (own(raw_requests) + head_total).astype(BF16)
    user_proj = mm(layer_out, user_full)

    owned = candidate_owner == cand_index
    table_rows = jnp.arange(cand_table.shape[0], dtype=jnp.int32)
    hits = owned[:, :, None] & (candidate_row[:, :, None] == table_rows)
    pre_score = user_proj[:, None, :] + item_proj[None]
    row_scores = jnp.sum(jax.nn.silu(pre_score) * score_weights, -1)
    scores = lax.psum(jnp.sum(jnp.where(hits, row_scores[:, None, :], 0.0), -1), "cand")
    log_total = jnp.log(jnp.sum(jnp.exp(scores), -1, keepdims=True))
    target = (relevance + 1).astype(F32)
    target = target / jnp.sum(target, -1, keepdims=True)
    losses = log_total[:, 0] - jnp.sum(target * scores, -1)
    d_score = jnp.exp(scores - log_total) - target
    row_grads = jnp.sum(jnp.where(hits, d_score[:, :, None], 0.0), 1)
    user_part = jnp.sum(row_grads[:, :, None] * silu_slope(pre_score), 1) * score_weights
    d_user = gather_user_grad(user_part)

    same = request_points[:, None] == request_points[None, :]
    order = jnp.arange(requests, dtype=jnp.int32)
    earlier = jnp.any(same & (order[None, :] < order[:, None]), 1)
    merge_same = (same & ~earlier[:, None]).astype(F32)
    d_user = jnp.dot(merge_same, d_user, precision=HIGHEST)
    d_picked = jnp.dot(d_user, user_full.astype(F32).T, precision=HIGHEST)
    d_gated = split(jnp.dot(d_picked, merge_weights.astype(F32).T, precision=HIGHEST))
    d_gate = (d_gated * normed).reshape(requests, cols)
    d_attended = norm_back(d_gated * gate_part, normed, inverse).astype(BF16)

    merge_cols = width // ctx_count
    own_picked = lax.dynamic_slice_in_dim(d_picked, ctx_index * merge_cols, merge_cols, 1)
    grad_merge = lax.dot_general(
        gated.astype(F32), own_picked, (((0,), (0,)), ((), ())), precision=HIGHEST
    )

    def own_features(array):
        return lax.dynamic_slice_in_dim(array, ctx_index * merge_cols, merge_cols, 1)

    def own_rows(array):
        return lax.dynamic_slice_in_dim(array, first_row, row_count, 0)

    def over_rows(rows, grads):
        return lax.dot_general(rows, grads, (((0,), (0,)), ((), ())), preferred_element_type=F32)

    positions = first_row + jnp.arange(row_count, dtype=jnp.int32)
    places = positions[:, None] == request_points[None, :]
    low_places = places.astype(BF16)
    x_own = own_features(x_low)
    x_own_requests = own_features(x_requests)
    head_grads = []
    own_grads = []
    for head in range(heads):
        span = slice(head * HEAD, (head + 1) * HEAD)
        slopes = back(d_attended[:, head], values[:, head])
        d_logit = jnp.where(
            allowed[0], slopes * silu_slope(logits[head]) / divisor[0], 0.0
        ).astype(BF16)
        d_query = mm(d_logit, key_heads[:, head]) * scaling
        d_key = over_rows(d_logit, queries[:, head]) * scaling
        d_value = over_rows(weight[head], d_attended[:, head])
        key_grad = (d_key * silu_slope(before_key[:, span])).astype(BF16)
        value_grad = (d_value * silu_slope(before_value[:, span])).astype(BF16)
        query_grad = (d_query * silu_slope(before_query[:, span])).astype(BF16)
        gate_grad = (d_gate[:, span] * silu_slope(before_gate[:, span])).astype(BF16)
        head_grads += [
            over_rows(x_own_requests, gate_grad),
            over_rows(x_own, value_grad),
            over_rows(x_own_requests, query_grad),
            over_rows(x_own, key_grad),
        ]
        own_grads += [
            mm(low_places, gate_grad).astype(BF16),
            own_rows(value_grad),
            mm(low_places, query_grad).astype(BF16),
            own_rows(key_grad),
        ]
    grad_heads = jnp.concatenate(head_grads, 1)
    d_normed = core_sum(back(jnp.concatenate(own_grads, 1), head_weights), 2)
    column_start = cand_index * slice_width
    d_input = lax.dynamic_slice_in_dim(
        norm_back(d_normed, x_normed, x_inverse), column_start, slice_width, 1
    )
    picked_cols = lax.dynamic_slice_in_dim(d_picked, column_start, slice_width, 1)
    d_layer = jnp.dot(places.astype(F32), picked_cols, precision=HIGHEST)
    history_grad = d_layer + d_input
    return (losses, history_grad, grad_heads, grad_merge)


def solution(mesh):
    return jax.shard_map(
        per_device,
        mesh=mesh,
        in_specs=(
            P("ctx", "cand"),
            P(None, "cand"),
            P("cand", None),
            P("cand", None),
            P("cand", None),
            P(),
            P(),
            P(),
            P("ctx", None),
            P("ctx", None),
            P("ctx", None),
        ),
        out_specs=(P("ctx"), P("ctx", "cand"), P("ctx", "cand"), P("cand", "ctx")),
        check_vma=False,
    )
```
